32 devices in a mesh: rep: 2 (over y), node: 4 (over z), local: 4 (over x, core).
Axes of the slice: x: 2, y: 2, z: 4, core: 2. Of those that a mesh axis runs over, the one named last changes fastest.
Arguments:
- tokens: bfloat16 [4096, 3584], P(('rep', 'node', 'local')), parts along dimension 0, may hold values from -6 to 6
- routes: int32 [4096, 2], P(('rep', 'node', 'local')), parts along dimension 0, may hold values from 0 to 7, all different within a row; in each aligned block of 128 rows (0 to 127, 128 to 255, ...) at most 40 rows name the same one
- gates: float32 [4096, 2], P(('rep', 'node', 'local')), parts along dimension 0, may hold values from 0.1 to 1.5
- placement: int32 [8], replicated, may hold values from 0 to 7, each once
- upstream: bfloat16 [4096, 3584], P(('rep', 'node', 'local')), parts along dimension 0, may hold values from -6 to 6
- w_gate: bfloat16 [16, 3584, 512], P(('node', 'local')), may hold values from -0.09375 to 0.09375
- w_up: bfloat16 [16, 3584, 512], P(('node', 'local')), may hold values from -0.09375 to 0.09375
- w_down: bfloat16 [16, 512, 3584], P(('node', 'local')), may hold values from -0.1875 to 0.1875
Outputs:
- grad_tokens: bfloat16 [4096, 3584], P(('rep', 'node', 'local')), parts along dimension 0
- grad_gates: float32 [4096, 2], P(('rep', 'node', 'local')), parts along dimension 0
The draws below stay inside these ranges and needn't reach their ends.
There are 2 independent parts, one for each index of `rep`. The reference program is written for one: setup_inputs(seed, part) draws one part's arguments, and reference() takes and returns one part's arrays. A program takes and returns all parts, laid end to end along the dimension named above; an argument that names none is the same for every part. Nothing has to cross between parts.
Inputs may be any that keep to these rules, and one draw needn't show every extreme that they name: `routes`: each row names 2 different experts; among the 128 rows of one device no expert is named by more than 40 rows, a bound that some block reaches. `placement`: A permutation of the slots.
All inputs are finite; a program needn't handle non-finite values.
Results may differ from the reference program's by a relative error of at most 0.015.
Values may be sent and summed in bfloat16 or wider, within the bound.
No kernel may reach another device: no remote copies, remote signals or barrier semaphores. Data moves between devices by JAX's collectives and lax.ppermute only.
A program may use at most 128 MiB of HBM per device.

```python
import math
import jax
import jax.numpy as jnp
import numpy as np
from jax import lax

D = 3584
HID = 1024
SLICES = 2
TOPK = 2
TOK_DEV = 128
HS = 512
EXPERTS = 8
PIECES = 16
MOST = 40
TOKENS = 2048
N_NODE = 4
N_LOCAL = 4


def levels(key, dims, cuts, least, largest):
    level, own = 1.0, jax.random.fold_in(key, 6)
    for position, parts in cuts:
        steps = jnp.exp(jax.random.uniform(jax.random.fold_in(own, position), (parts,), jnp.float32, least / len(cuts), largest / len(cuts)))
        level = level * jnp.repeat(steps, dims[position] // parts).reshape([-1 if axis == position else 1 for axis in range(len(dims))])
    return level


def deal_out(own_key, own, number, rows, amount, top, limit, slope):
    sequence = jax.random.permutation(own_key, amount)
    heavy_load, common = portions_of(amount, rows * top, limit, slope, True), portions_of(amount, rows * top, limit, slope, False)
    places = jnp.arange(amount)

    def named(lengths, rotation):
        used = int((lengths > 0).sum())
        fixed = max(1, used // 4)
        shifted = fixed + (places - fixed + rotation * (used - fixed)) % max(1, amount - fixed)
        return jnp.zeros((amount,), jnp.int32).at[sequence[jnp.where(places < fixed, places, shifted)]].set(jnp.asarray(lengths, jnp.int32))

    lengths = jnp.where(number % 4 == 0, named(heavy_load, number // 4), named(common, number - number // 4 - 1))
    mixed = jax.random.permutation(jax.random.fold_in(own, 3), amount)
    donor, receiver = mixed[0:amount // 2 * 2:2], mixed[1:amount // 2 * 2:2]
    margin = jnp.minimum(lengths[donor] - 1, limit - lengths[receiver]) // 2
    margin = jnp.where((donor == sequence[0]) | (receiver == sequence[0]) | (lengths[receiver] == 0), 0, jnp.maximum(margin, 0))
    shifted = jax.random.randint(jax.random.fold_in(own, 4), (amount // 2,), 0, 1 << 20) % (margin + 1)
    lengths = lengths.at[donor].add(-shifted).at[receiver].add(shifted)
    items = jnp.searchsorted(jnp.cumsum(lengths), jnp.arange(rows * top), side="right").astype(jnp.int32)
    table = items.reshape(top, rows).T
    table = table[jax.random.permutation(jax.random.fold_in(own, 1), rows)]
    rotation = jax.random.randint(jax.random.fold_in(own, 2), (rows, 1), 0, top)
    return jnp.take_along_axis(table, (jnp.arange(top)[None, :] + rotation) % top, axis=1)


def portions_of(count, total, reach, lean, full):
    weights = [(1 << 20) // math.isqrt(standing ** lean) + 1 for standing in range(1, count + 1)]
    largest = reach if full else min(reach, max(-(-total // count), total * weights[0] // sum(weights)))
    least = 1 if total - largest >= count - 1 else 0
    given, surplus = [largest] + [least] * (count - 1), total - largest - least * (count - 1)
    while surplus > 0:
        free = [i for i in range(1, count) if given[i] < largest] or [i for i in range(1, count) if given[i] < reach]
        pool, budget = sum([weights[i] for i in free]), surplus
        for i in free:
            more = min(reach - given[i], max(1, budget * weights[i] // pool), surplus)
            given[i] = given[i] + more
            surplus = surplus - more
    return np.array(given)


def noise(rng, extent, deviation, bound, shards=(), kind=jnp.bfloat16):
    gain = levels(rng, extent, shards, -0.22, 0.18) if shards else 1.0
    result = jax.random.normal(rng, extent, jnp.float32) * deviation * gain
    return jnp.minimum(jnp.maximum(result, -bound), bound).astype(kind)


def setup_inputs(seed: int = 0, part: int = 0) -> dict:
    seeds = jax.random.split(jax.random.key(seed), 9)
    part_keys = jax.random.split(jax.random.fold_in(seeds[8], part), 9)
    tokens = noise(part_keys[0], (TOKENS, D), 1.0, 6.0, ((0, 16),))
    routes_keys = jax.random.split(jax.random.fold_in(part_keys[1], 1), TOKENS // TOK_DEV)
    routes_turns = jax.random.permutation(jax.random.fold_in(part_keys[1], 3), TOKENS // TOK_DEV)
    routes = jax.vmap(lambda own, number: deal_out(jax.random.fold_in(part_keys[1], 2), own, number, TOK_DEV, EXPERTS, TOPK, MOST, 2))(routes_keys, routes_turns).reshape((TOKENS, TOPK))
    gates = jnp.clip(jnp.exp(math.log(1.5) - 2.7080502 * jax.random.uniform(part_keys[2], (TOKENS, TOPK), jnp.float32) ** levels(part_keys[2], (TOKENS, TOPK), ((0, 16),), -0.2, 0.2)), 0.1, 1.5)
    placement = jax.random.permutation(seeds[3], EXPERTS).astype(jnp.int32)
    upstream = noise(part_keys[4], (TOKENS, D), 1.0, 6.0, ((0, 16),))
    w_gate = noise(seeds[5], (PIECES, D, HS), D ** -0.5, 0.09375, ((0, 16),))
    w_up = noise(seeds[6], (PIECES, D, HS), D ** -0.5, 0.09375, ((0, 16),))
    w_down = noise(seeds[7], (PIECES, HS, D), HID ** -0.5, 0.1875, ((0, 16),))
    return {"tokens": tokens, "routes": routes, "gates": gates, "placement": placement, "upstream": upstream, "w_gate": w_gate, "w_up": w_up, "w_down": w_down}


def expert_piece(got_tokens, got_upstream, gate_col, gate_piece, up_piece, down_piece):
    gate_lin = jnp.dot(got_tokens, gate_piece, preferred_element_type=jnp.float32)
    up_lin = jnp.dot(got_tokens, up_piece, preferred_element_type=jnp.float32)
    sigmoid_g = jax.nn.sigmoid(gate_lin)
    activated = gate_lin * sigmoid_g
    hidden = (activated * up_lin).astype(jnp.bfloat16)
    projected = lax.dot_general(got_upstream, down_piece, (((1,), (1,)), ((), ())), preferred_element_type=jnp.float32)
    part_grad = jnp.sum(projected * hidden.astype(jnp.float32), axis=1)
    grad_hidden = gate_col[:, None] * projected
    d_gate = (grad_hidden * up_lin * sigmoid_g * (1.0 + gate_lin * (1.0 - sigmoid_g))).astype(jnp.bfloat16)
    d_up = (grad_hidden * activated).astype(jnp.bfloat16)
    piece_grad = lax.dot_general(d_gate, gate_piece, (((1,), (1,)), ((), ())), preferred_element_type=jnp.float32)
    piece_grad = piece_grad + lax.dot_general(d_up, up_piece, (((1,), (1,)), ((), ())), preferred_element_type=jnp.float32)
    return piece_grad.astype(jnp.bfloat16), part_grad


def reference(tokens, routes, gates, placement, upstream, w_gate, w_up, w_down):
    flat_expert = routes.reshape(-1).astype(jnp.int32)
    flat_gate = gates.reshape(-1)
    capacity = N_NODE * N_LOCAL * MOST
    inverse = jnp.argsort(placement).astype(jnp.int32)

    def per_slot(carry, slot_index):
        acc_tokens, acc_gates = carry
        expert = inverse[slot_index]
        missing = (flat_expert != expert).astype(jnp.int32)
        ordering = jnp.argsort(missing, stable=True)[:capacity].astype(jnp.int32)
        is_valid = missing[ordering] == 0
        token_index = ordering // TOPK
        got_tokens = tokens[token_index]
        got_upstream = upstream[token_index]
        gate_col = jnp.where(is_valid, flat_gate[ordering], jnp.float32(0.0))
        start = (slot_index * SLICES).astype(jnp.int32)
        gate_all = lax.dynamic_slice_in_dim(w_gate, start, SLICES, 0)
        up_all = lax.dynamic_slice_in_dim(w_up, start, SLICES, 0)
        down_all = lax.dynamic_slice_in_dim(w_down, start, SLICES, 0)
        grad_sum = jnp.zeros((capacity, D), jnp.float32)
        gate_sum = jnp.zeros((capacity,), jnp.float32)
        for part_index in range(SLICES):
            piece_grad, part_grad = expert_piece(got_tokens, got_upstream, gate_col, gate_all[part_index], up_all[part_index], down_all[part_index])
            grad_sum = grad_sum + piece_grad.astype(jnp.float32)
            gate_sum = gate_sum + part_grad
        expert_grad = grad_sum.astype(jnp.bfloat16).astype(jnp.float32) * is_valid[:, None].astype(jnp.float32)
        acc_tokens = acc_tokens.at[token_index].add(expert_grad)
        acc_gates = acc_gates.at[ordering].add(jnp.where(is_valid, gate_sum, jnp.float32(0.0)))
        return (acc_tokens, acc_gates), None

    start_carry = (jnp.zeros((TOKENS, D), jnp.float32), jnp.zeros((TOKENS * TOPK,), jnp.float32))
    (acc_tokens, acc_gates), _ = lax.scan(per_slot, start_carry, jnp.arange(EXPERTS, dtype=jnp.int32))
    return acc_tokens.astype(jnp.bfloat16), acc_gates.reshape(TOKENS, TOPK)
```

```python
import jax
import jax.numpy as jnp
from jax import lax
from jax.sharding import Mesh
from jax.sharding import PartitionSpec as P

BF16 = jnp.bfloat16
F32 = jnp.float32
CHIPS = ("node", "chip")
ROWS = ("rep", "node", "chip", "core")
PIECES = ("node", "chip", "core")


def nt(left, right):
    return lax.dot_general(left, right, (((1,), (1,)), ((), ())), preferred_element_type=F32)


def nn(left, right):
    return jnp.dot(left, right, preferred_element_type=F32)


def forward_lins(rows, gate_piece, up_piece):
    return nn(rows, gate_piece), nn(rows, up_piece)


def backward_lins(gate_lin, up_lin, projected):
    sigmoid_g = jax.nn.sigmoid(gate_lin)
    activated = gate_lin * sigmoid_g
    hidden = (activated * up_lin).astype(BF16).astype(F32)
    part_grad = jnp.sum(projected * hidden, axis=1)
    d_gate = (projected * up_lin * sigmoid_g * (1.0 + gate_lin * (1.0 - sigmoid_g))).astype(BF16)
    d_up = (projected * activated).astype(BF16)
    return d_gate, d_up, part_grad


def swap_cores(values):
    return lax.ppermute(values, "core", [(0, 1), (1, 0)])


def to_chips(values):
    return lax.all_to_all(values, CHIPS, split_axis=0, concat_axis=0, tiled=True)


def per_device(tokens, routes, gates, placement, upstream, w_gate, w_up, w_down):
    tok_dev, width = tokens.shape
    top_count = routes.shape[1]
    experts = placement.shape[0]
    capacity = 5 * tok_dev * top_count // (4 * experts)
    nrows = experts * capacity
    hit = (routes[:, :, None] == jnp.arange(experts, dtype=jnp.int32)).astype(jnp.int32)
    named = jnp.sum(hit, axis=1)
    before = jnp.cumsum(named, axis=0) - named
    rank = jnp.sum(hit * before[:, None, :], axis=2)
    slot = jnp.sum(hit * placement, axis=2)
    row_index = slot * capacity + rank
    rows = jnp.arange(nrows, dtype=jnp.int32)
    pair_hit = rows[:, None, None] == row_index.T[None]
    dispatch = jnp.any(pair_hit, axis=1).astype(BF16)

    sent_tokens = nn(dispatch, tokens).astype(BF16).reshape(experts, capacity, width)
    sent_upstream = nn(dispatch, upstream).astype(BF16).reshape(experts, capacity, width)
    own_tokens = to_chips(sent_tokens).reshape(nrows, width)
    own_upstream = to_chips(sent_upstream).reshape(nrows, width)
    other_tokens = swap_cores(own_tokens)
    other_upstream = swap_cores(own_upstream)

    gate_piece, up_piece, down_piece = w_gate[0], w_up[0], w_down[0]

    def piece(got_tokens, got_upstream):
        gate_lin, up_lin = forward_lins(got_tokens, gate_piece, up_piece)
        d_gate, d_up, part = backward_lins(gate_lin, up_lin, nt(got_upstream, down_piece))
        return (nt(d_gate, gate_piece) + nt(d_up, up_piece)).astype(BF16), part

    other_grad, other_part = piece(other_tokens, other_upstream)
    own_grad, own_part = piece(own_tokens, own_upstream)
    expert_grad = (own_grad.astype(F32) + swap_cores(other_grad).astype(F32)).astype(BF16)
    part_sum = own_part + swap_cores(other_part)

    back_grad = to_chips(expert_grad.reshape(experts, capacity, width)).reshape(nrows, width)
    parts = lax.all_gather(part_sum.reshape(experts, capacity), CHIPS, axis=0, tiled=False)
    chip = lax.axis_index("node") * lax.axis_size("chip") + lax.axis_index("chip")
    back_part = lax.dynamic_index_in_dim(parts, chip, axis=1, keepdims=False).reshape(nrows)

    grad_gates = jnp.sum(jnp.where(pair_hit, back_part[:, None, None], 0.0), axis=0).T
    combine = jnp.sum(jnp.where(pair_hit, gates.T[None], 0.0), axis=1)
    weighted = combine.T
    high = weighted.astype(BF16)
    low = (weighted - high.astype(F32)).astype(BF16)
    grad_tokens = (nn(high, back_grad) + nn(low, back_grad)).astype(BF16)
    return grad_tokens, grad_gates


def solution(mesh):
    shape = mesh.devices.shape
    split = Mesh(
        mesh.devices.reshape(shape[0], shape[1], shape[2] // 2, 2), ("rep", "node", "chip", "core")
    )
    return jax.shard_map(
        per_device,
        mesh=split,
        in_specs=(
            P(ROWS, None),
            P(ROWS, None),
            P(ROWS, None),
            P(),
            P(ROWS, None),
            P(PIECES, None, None),
            P(PIECES, None, None),
            P(PIECES, None, None),
        ),
        out_specs=(P(ROWS, None), P(ROWS, None)),
        check_vma=False,
    )
```

```python
import functools

import jax
import jax.numpy as jnp
from jax import lax
from jax.experimental import pallas as pl
from jax.experimental.pallas import tpu as pltpu
from jax.sharding import Mesh
from jax.sharding import PartitionSpec as P

BF16 = jnp.bfloat16
F32 = jnp.float32
CHIPS = ("node", "chip")
ROWS = ("rep", "node", "chip", "core")
PIECES = ("node", "chip", "core")
LANES = 128
VMEM = pl.BlockSpec(memory_space=pltpu.VMEM)
SMALL = pl.CostEstimate(flops=1, bytes_accessed=1, transcendentals=0)


def nt(left, right):
    return lax.dot_general(left, right, (((1,), (1,)), ((), ())), preferred_element_type=F32)


def nn(left, right):
    return jnp.dot(left, right, preferred_element_type=F32)


def swap_cores(values):
    return lax.ppermute(values, "core", [(0, 1), (1, 0)])


def dispatch_kernel(offsets, capacity, index_ref, tokens_ref, upstream_ref, *out_refs):
    count = tokens_ref.shape[0]
    for offset, out_ref in zip(offsets, out_refs):
        rows = lax.broadcasted_iota(jnp.int32, (capacity, count), 0) + offset * capacity
        hits = jnp.zeros((capacity, count), F32)
        for choice in range(index_ref.shape[0]):
            hits = hits + jnp.where(rows == index_ref[choice : choice + 1, :], 1.0, 0.0)
        hits = hits.astype(BF16)
        out_ref[0] = nn(hits, tokens_ref[...]).astype(BF16)
        out_ref[1] = nn(hits, upstream_ref[...]).astype(BF16)


def dispatch(row_index, tokens, upstream, offsets, capacity):
    width = tokens.shape[1]
    return pl.pallas_call(
        functools.partial(dispatch_kernel, offsets, capacity),
        out_shape=[jax.ShapeDtypeStruct((2, capacity, width), BF16)] * len(offsets),
        in_specs=[VMEM] * 3,
        out_specs=[VMEM] * len(offsets),
        compiler_params=pltpu.CompilerParams(vmem_limit_bytes=48 << 20),
        cost_estimate=SMALL,
        name="dispatch",
    )(row_index, tokens, upstream)


def expert_kernel(tiles, tokens_ref, upstream_ref, *refs):
    own_refs, other_refs, (out_ref, total, part) = refs[:3], refs[3:6], refs[6:]
    step = pl.program_id(0)
    width = tokens_ref.shape[1]

    @pl.when(step == 0)
    def _():
        total[...] = jnp.zeros_like(total)
        part[...] = jnp.zeros_like(part)

    def tile(gate_ref, up_ref, down_ref):
        tokens = tokens_ref[...]
        gate_piece, up_piece = gate_ref[0], up_ref[0]
        gate_lin = nn(tokens, gate_piece)
        up_lin = nn(tokens, up_piece)
        projected = nt(upstream_ref[...], down_ref[0])
        sigmoid_g = jax.nn.sigmoid(gate_lin)
        activated = gate_lin * sigmoid_g
        hidden = (activated * up_lin).astype(BF16).astype(F32)
        part[...] += jnp.sum(projected * hidden, axis=1, keepdims=True)
        slope = sigmoid_g * (1.0 + gate_lin * (1.0 - sigmoid_g))
        d_gate = (projected * up_lin * slope).astype(BF16)
        d_up = (projected * activated).astype(BF16)
        total[...] += nt(d_gate, gate_piece) + nt(d_up, up_piece)

    pl.when(step < tiles)(lambda: tile(*own_refs))
    pl.when(step >= tiles)(lambda: tile(*other_refs))

    @pl.when(step == pl.num_programs(0) - 1)
    def _():
        out_ref[:, :width] = total[...].astype(BF16)
        out_ref[:, width:] = jnp.broadcast_to(part[...], (part.shape[0], LANES)).astype(BF16)


def expert(tokens, upstream, own, other):
    rows, width = tokens.shape
    hidden = own[0].shape[2]
    tile = min(256, hidden)
    tiles = hidden // tile

    def weights(place):
        return [
            pl.BlockSpec((1, width, tile), lambda h: (0, 0, place(h))),
            pl.BlockSpec((1, width, tile), lambda h: (0, 0, place(h))),
            pl.BlockSpec((1, tile, width), lambda h: (0, place(h), 0)),
        ]

    return pl.pallas_call(
        functools.partial(expert_kernel, tiles),
        out_shape=jax.ShapeDtypeStruct((rows, width + LANES), BF16),
        grid=(2 * tiles,),
        in_specs=[pl.BlockSpec((rows, width), lambda h: (0, 0))] * 2
        + weights(lambda h: jnp.minimum(h, tiles - 1))
        + weights(lambda h: jnp.maximum(h - tiles, 0)),
        out_specs=pl.BlockSpec((rows, width + LANES), lambda h: (0, 0)),
        scratch_shapes=[pltpu.VMEM((rows, width), F32), pltpu.VMEM((rows, 1), F32)],
        compiler_params=pltpu.CompilerParams(vmem_limit_bytes=56 << 20),
        cost_estimate=SMALL,
        name="expert",
    )(tokens, upstream, *own, *other)


def per_device(tokens, routes, gates, placement, upstream, w_gate, w_up, w_down):
    tok_dev, width = tokens.shape
    top_count = routes.shape[1]
    experts = placement.shape[0]
    nodes, node_chips = lax.axis_size("node"), lax.axis_size("chip")
    chips = nodes * node_chips
    assert chips == experts and chips & (chips - 1) == 0 and nodes % 4 == 0
    capacity = 5 * tok_dev * top_count // (4 * experts)
    me = lax.axis_index("node") * node_chips + lax.axis_index("chip")

    hit = (routes[:, :, None] == jnp.arange(experts, dtype=jnp.int32)).astype(jnp.int32)
    named = jnp.sum(hit, axis=1)
    before = jnp.cumsum(named, axis=0) - named
    rank = jnp.sum(hit * before[:, None, :], axis=2)
    slot = jnp.sum(hit * placement, axis=2)
    row_index = ((slot ^ me) * capacity + rank).T

    def move(sent, offsets):
        return [
            lax.ppermute(rows, CHIPS, [(i, i ^ offset) for i in range(chips)]) if offset else rows
            for rows, offset in zip(sent, offsets)
        ]

    def work(got, weights):
        both = jnp.stack(got, axis=1).reshape(2, len(got) * capacity, width)
        out = expert(both[0], both[1], *weights)
        return [out[i * capacity : (i + 1) * capacity] for i in range(len(got))]

    def combine(back, offsets):
        rows = jnp.arange(capacity, dtype=jnp.int32)
        hits = jnp.concatenate(
            [(rows + o * capacity)[:, None, None] == row_index[None] for o in offsets]
        )
        weighted = jnp.sum(jnp.where(hits, gates.T[None], 0.0), axis=1).T
        high = weighted.astype(BF16)
        low = (weighted - high.astype(F32)).astype(BF16)
        rows = jnp.concatenate(back)
        part = rows[:, width].astype(F32)
        rows = rows[:, :width]
        return nn(high, rows) + nn(low, rows), jnp.sum(
            jnp.where(hits, part[:, None, None], 0.0), axis=0
        ).T

    near1 = list(range(3 * chips // 8))
    near2 = list(range(3 * chips // 8, chips // 2))
    far1 = list(range(chips // 2, 3 * chips // 4))
    far2 = list(range(3 * chips // 4, chips))
    half = len(far1) // 2
    tie = lax.optimization_barrier

    s_far1 = dispatch(row_index, tokens, upstream, far1, capacity)
    row_index_later, s_far1 = tie((row_index, s_far1))
    s_rest = dispatch(row_index_later, tokens, upstream, far2 + near1 + near2, capacity)
    s_far2, s_near1 = s_rest[: len(far2)], s_rest[len(far2) : len(far2) + len(near1)]
    s_near2 = s_rest[len(far2) + len(near1) :]
    own = (w_gate, w_up, w_down)
    d_far1 = move(s_far1, far1)
    other = tuple(swap_cores(piece) for piece in own)
    s_near1, other = tie((s_near1, other))
    d_near1 = move(s_near1, near1)

    d_far1, d_near1, s_far2, s_near2 = tie((d_far1, d_near1, s_far2, s_near2))
    d_far2 = move(s_far2, far2)
    d_near2 = move(s_near2, near2)
    first = work(d_far1 + d_near1, (own, other))
    b_near1 = move(first[len(far1) :], near1)
    d_far2, d_near2, first, b_near1 = tie((d_far2, d_near2, first, b_near1))

    b_far1 = move(first[: len(far1)], far1)
    second = work(d_far2 + d_near2, (own, other))
    b_far1, second = tie((b_far1, second))

    second = move(second, far2 + near2)
    early, gate_early = combine(b_far1 + b_near1, far1 + near1)
    late, gate_late = combine(second, far2 + near2)
    return (early + late).astype(BF16), gate_early + gate_late


def solution(mesh):
    shape = mesh.devices.shape
    split = Mesh(
        mesh.devices.reshape(shape[0], shape[1], shape[2] // 2, 2), ("rep", "node", "chip", "core")
    )
    return jax.shard_map(
        per_device,
        mesh=split,
        in_specs=(
            P(ROWS, None),
            P(ROWS, None),
            P(ROWS, None),
            P(),
            P(ROWS, None),
            P(PIECES, None, None),
            P(PIECES, None, None),
            P(PIECES, None, None),
        ),
        out_specs=(P(ROWS, None), P(ROWS, None)),
        check_vma=False,
    )
```

```python
import functools

import jax
import jax.numpy as jnp
from jax import lax
from jax.experimental import pallas as pl
from jax.experimental.pallas import tpu as pltpu
from jax.sharding import Mesh
from jax.sharding import PartitionSpec as P

BF16 = jnp.bfloat16
F32 = jnp.float32
CHIPS = ("node", "chip")
ROWS = ("rep", "node", "chip", "core")
PIECES = ("node", "chip", "core")
LANES = 128
VMEM = pl.BlockSpec(memory_space=pltpu.VMEM)
SMALL = pl.CostEstimate(flops=1, bytes_accessed=1, transcendentals=0)


def nt(left, right):
    return lax.dot_general(left, right, (((1,), (1,)), ((), ())), preferred_element_type=F32)


def nn(left, right):
    return jnp.dot(left, right, preferred_element_type=F32)


def swap_cores(values):
    return lax.ppermute(values, "core", [(0, 1), (1, 0)])


def dispatch_kernel(offsets, capacity, index_ref, *refs):
    sources, out_refs = refs[: -len(offsets)], refs[-len(offsets) :]
    count = index_ref.shape[1]
    for offset, out_ref in zip(offsets, out_refs):
        rows = lax.broadcasted_iota(jnp.int32, (capacity, count), 0) + offset * capacity
        hits = jnp.zeros((capacity, count), F32)
        for choice in range(index_ref.shape[0]):
            hits = hits + jnp.where(rows == index_ref[choice : choice + 1, :], 1.0, 0.0)
        hits = hits.astype(BF16)
        for place, source in enumerate(sources):
            out_ref[place] = nn(hits, source[...]).astype(BF16)


def dispatch(row_index, sources, offsets, capacity):
    width = sources[0].shape[1]
    shape = (len(sources), capacity, width)
    return pl.pallas_call(
        functools.partial(dispatch_kernel, offsets, capacity),
        out_shape=[jax.ShapeDtypeStruct(shape, BF16)] * len(offsets),
        in_specs=[VMEM] * (1 + len(sources)),
        out_specs=[VMEM] * len(offsets),
        compiler_params=pltpu.CompilerParams(vmem_limit_bytes=48 << 20),
        cost_estimate=SMALL,
        name="dispatch",
    )(row_index, *sources)


def expert_kernel(tile, tokens_ref, upstream_ref, *refs):
    pieces, (out_ref, total, part) = (refs[:3], refs[3:6]), refs[6:]
    width = tokens_ref.shape[1]
    total[...] = jnp.zeros_like(total)
    part[...] = jnp.zeros_like(part)
    for gate_ref, up_ref, down_ref in pieces:
        for start in range(0, gate_ref.shape[2], tile):
            units = slice(start, start + tile)
            tokens = tokens_ref[...]
            gate_piece, up_piece = gate_ref[0, :, units], up_ref[0, :, units]
            gate_lin = nn(tokens, gate_piece)
            up_lin = nn(tokens, up_piece)
            projected = nt(upstream_ref[...], down_ref[0, units, :])
            sigmoid_g = jax.nn.sigmoid(gate_lin)
            activated = gate_lin * sigmoid_g
            hidden = (activated * up_lin).astype(BF16).astype(F32)
            part[...] += jnp.sum(projected * hidden, axis=1, keepdims=True)
            slope = sigmoid_g * (1.0 + gate_lin * (1.0 - sigmoid_g))
            d_gate = (projected * up_lin * slope).astype(BF16)
            d_up = (projected * activated).astype(BF16)
            total[...] += nt(d_gate, gate_piece) + nt(d_up, up_piece)
    out_ref[:, :width] = total[...].astype(BF16)
    out_ref[:, width:] = jnp.broadcast_to(part[...], (part.shape[0], LANES)).astype(BF16)


def expert(tokens, upstream, own, other):
    rows, width = tokens.shape
    return pl.pallas_call(
        functools.partial(expert_kernel, min(256, own[0].shape[2])),
        out_shape=jax.ShapeDtypeStruct((rows, width + LANES), BF16),
        in_specs=[VMEM] * 8,
        out_specs=VMEM,
        scratch_shapes=[pltpu.VMEM((rows, width), F32), pltpu.VMEM((rows, 1), F32)],
        compiler_params=pltpu.CompilerParams(vmem_limit_bytes=38 << 20),
        cost_estimate=SMALL,
        name="expert",
    )(tokens, upstream, *own, *other)


def per_device(tokens, routes, gates, placement, upstream, w_gate, w_up, w_down):
    tok_dev, width = tokens.shape
    top_count = routes.shape[1]
    experts = placement.shape[0]
    nodes, node_chips = lax.axis_size("node"), lax.axis_size("chip")
    chips = nodes * node_chips
    assert chips == experts and chips & (chips - 1) == 0 and nodes % 4 == 0
    capacity = 5 * tok_dev * top_count // (4 * experts)
    me = lax.axis_index("node") * node_chips + lax.axis_index("chip")

    hit = (routes[:, :, None] == jnp.arange(experts, dtype=jnp.int32)).astype(jnp.int32)
    named = jnp.sum(hit, axis=1)
    before = jnp.cumsum(named, axis=0) - named
    rank = jnp.sum(hit * before[:, None, :], axis=2)
    slot = jnp.sum(hit * placement, axis=2)
    row_index = ((slot ^ me) * capacity + rank).T

    def move(sent, offsets):
        return [
            lax.ppermute(rows, CHIPS, [(i, i ^ offset) for i in range(chips)]) if offset else rows
            for rows, offset in zip(sent, offsets)
        ]

    def work(got_tokens, got_upstream, weights):
        out = expert(jnp.concatenate(got_tokens), jnp.concatenate(got_upstream), *weights)
        return [out[i * capacity : (i + 1) * capacity] for i in range(len(got_tokens))]

    def combine(back, offsets):
        rows = jnp.arange(capacity, dtype=jnp.int32)
        hits = jnp.concatenate(
            [(rows + o * capacity)[:, None, None] == row_index[None] for o in offsets]
        )
        weighted = jnp.sum(jnp.where(hits, gates.T[None], 0.0), axis=1).T
        high = weighted.astype(BF16)
        low = (weighted - high.astype(F32)).astype(BF16)
        rows = jnp.concatenate(back)
        part = rows[:, width].astype(F32)
        rows = rows[:, :width]
        return nn(high, rows) + nn(low, rows), jnp.sum(
            jnp.where(hits, part[:, None, None], 0.0), axis=0
        ).T

    half = chips // 2
    near = list(range(half))
    far1, far2 = list(range(half, half + half // 2)), list(range(half + half // 2, chips))
    side = list(range(half // 2))
    cross = list(range(half // 2, half))
    tie = lax.optimization_barrier
    weights = ((w_gate, w_up, w_down), tuple(swap_cores(piece) for piece in (w_gate, w_up, w_down)))

    mirror_tokens = move([tokens], [half])[0]
    sent = dispatch(row_index, [tokens, upstream], near, capacity)
    sent_far = [rows[0] for rows in dispatch(row_index, [upstream], far1 + far2, capacity)]
    sent_side, sent_cross = sent[: len(side)], sent[len(side) :]
    sent_side, index, weights = tie((sent_side, row_index, weights))
    cut = len(cross) // 2
    got_side = move(sent_side, side)
    got_cross = move(sent_cross[:cut], cross[:cut])
    mirror_index = move([index], [half])[0]

    first_up, mirror_tokens = tie((sent_far[:cut], mirror_tokens))
    up_far1 = move(first_up, far1[:cut])
    mirror_tokens, mirror_index, got_cross, got_side, sent_last, rest_up = tie(
        (mirror_tokens, mirror_index, got_cross, got_side, sent_cross[cut:], sent_far[cut:])
    )
    up_far1 += move(rest_up[: len(far1) - cut], far1[cut:])
    sent_far = rest_up[len(far1) - cut :]
    passed = [rows[0] for rows in dispatch(mirror_index, [mirror_tokens], far1 + far2, capacity)]
    pass_far1 = move(passed[: len(far1)], side)
    got_cross += move(sent_last, cross[cut:])
    up_far1, sent_far = tie((up_far1, sent_far))
    up_far2 = move(sent_far, far2)
    up_far1, pass_far1, got_side, got_cross, passed = tie(
        (up_far1, pass_far1, got_side, got_cross, passed[len(far1) :])
    )
    pass_far2 = move(passed, cross)
    got = got_side + got_cross
    first = work(
        pass_far1 + [rows[0] for rows in got], up_far1 + [rows[1] for rows in got], weights
    )
    up_far2, pass_far2, first = tie((up_far2, pass_far2, first))
    back_far1 = move(first[: len(far1)], far1)
    back_near = move(first[len(far1) :], near)
    second = work(pass_far2, up_far2, weights)
    back_far1, second = tie((back_far1, second))
    back_far2 = move(second, far2)
    early, gate_early = combine(back_far1, far1)
    late, gate_late = combine(back_far2 + back_near, far2 + near)
    return (early + late).astype(BF16), gate_early + gate_late


def solution(mesh):
    shape = mesh.devices.shape
    split = Mesh(
        mesh.devices.reshape(shape[0], shape[1], shape[2] // 2, 2), ("rep", "node", "chip", "core")
    )
    return jax.shard_map(
        per_device,
        mesh=split,
        in_specs=(
            P(ROWS, None),
            P(ROWS, None),
            P(ROWS, None),
            P(),
            P(ROWS, None),
            P(PIECES, None, None),
            P(PIECES, None, None),
            P(PIECES, None, None),
        ),
        out_specs=(P(ROWS, None), P(ROWS, None)),
        check_vma=False,
    )
```

```python
import functools

import jax
import jax.numpy as jnp
from jax import lax
from jax.experimental import pallas as pl
from jax.experimental.pallas import tpu as pltpu
from jax.sharding import Mesh
from jax.sharding import PartitionSpec as P

BF16 = jnp.bfloat16
F32 = jnp.float32
CHIPS = ("node", "chip")
ROWS = ("rep", "node", "chip", "core")
PIECES = ("node", "chip", "core")
LANES = 128
VMEM = pl.BlockSpec(memory_space=pltpu.VMEM)
SMALL = pl.CostEstimate(flops=1, bytes_accessed=1, transcendentals=0)


def nt(left, right):
    return lax.dot_general(left, right, (((1,), (1,)), ((), ())), preferred_element_type=F32)


def nn(left, right):
    return jnp.dot(left, right, preferred_element_type=F32)


def swap_cores(values):
    return lax.ppermute(values, "core", [(0, 1), (1, 0)])


def dispatch_kernel(offsets, capacity, index_ref, *refs):
    sources, out_refs = refs[: -len(offsets)], refs[-len(offsets) :]
    count = index_ref.shape[1]
    for offset, out_ref in zip(offsets, out_refs):
        rows = lax.broadcasted_iota(jnp.int32, (capacity, count), 0) + offset * capacity
        hits = jnp.zeros((capacity, count), F32)
        for choice in range(index_ref.shape[0]):
            hits = hits + jnp.where(rows == index_ref[choice : choice + 1, :], 1.0, 0.0)
        hits = hits.astype(BF16)
        for place, source in enumerate(sources):
            out_ref[place] = nn(hits, source[...]).astype(BF16)


def dispatch(row_index, sources, offsets, capacity):
    width = sources[0].shape[1]
    shape = (len(sources), capacity, width)
    return pl.pallas_call(
        functools.partial(dispatch_kernel, offsets, capacity),
        out_shape=[jax.ShapeDtypeStruct(shape, BF16)] * len(offsets),
        in_specs=[VMEM] * (1 + len(sources)),
        out_specs=[VMEM] * len(offsets),
        compiler_params=pltpu.CompilerParams(vmem_limit_bytes=48 << 20),
        cost_estimate=SMALL,
        name="dispatch",
    )(row_index, *sources)


def expert_kernel(tile, tokens_ref, upstream_ref, *refs):
    pieces, out_refs, (total, part) = (refs[:3], refs[3:6]), refs[6:-2], refs[-2:]
    width = tokens_ref.shape[1]
    total[...] = jnp.zeros_like(total)
    part[...] = jnp.zeros_like(part)
    for gate_ref, up_ref, down_ref in pieces:
        for start in range(0, gate_ref.shape[2], tile):
            units = slice(start, start + tile)
            tokens = tokens_ref[...]
            gate_piece, up_piece = gate_ref[0, :, units], up_ref[0, :, units]
            gate_lin = nn(tokens, gate_piece)
            up_lin = nn(tokens, up_piece)
            projected = nt(upstream_ref[...], down_ref[0, units, :])
            sigmoid_g = jax.nn.sigmoid(gate_lin)
            activated = gate_lin * sigmoid_g
            hidden = (activated * up_lin).astype(BF16).astype(F32)
            part[...] += jnp.sum(projected * hidden, axis=1, keepdims=True)
            slope = sigmoid_g * (1.0 + gate_lin * (1.0 - sigmoid_g))
            d_gate = (projected * up_lin * slope).astype(BF16)
            d_up = (projected * activated).astype(BF16)
            total[...] += nt(d_gate, gate_piece) + nt(d_up, up_piece)
    for place, out_ref in enumerate(out_refs):
        count = out_ref.shape[0]
        rows = slice(place * count, (place + 1) * count)
        out_ref[:, :width] = total[rows, :].astype(BF16)
        out_ref[:, width:] = jnp.broadcast_to(part[rows, :], (count, LANES)).astype(BF16)


def expert(tokens, upstream, own, other, blocks):
    rows, width = tokens.shape
    return pl.pallas_call(
        functools.partial(expert_kernel, min(256, own[0].shape[2])),
        out_shape=[jax.ShapeDtypeStruct((rows // blocks, width + LANES), BF16)] * blocks,
        in_specs=[VMEM] * 8,
        out_specs=[VMEM] * blocks,
        scratch_shapes=[pltpu.VMEM((rows, width), F32), pltpu.VMEM((rows, 1), F32)],
        compiler_params=pltpu.CompilerParams(vmem_limit_bytes=38 << 20),
        cost_estimate=SMALL,
        name="expert",
    )(tokens, upstream, *own, *other)


def per_device(tokens, routes, gates, placement, upstream, w_gate, w_up, w_down):
    tok_dev, width = tokens.shape
    top_count = routes.shape[1]
    experts = placement.shape[0]
    nodes, node_chips = lax.axis_size("node"), lax.axis_size("chip")
    chips = nodes * node_chips
    assert chips == experts and chips & (chips - 1) == 0 and nodes % 4 == 0
    capacity = 5 * tok_dev * top_count // (4 * experts)
    me = lax.axis_index("node") * node_chips + lax.axis_index("chip")

    hit = (routes[:, :, None] == jnp.arange(experts, dtype=jnp.int32)).astype(jnp.int32)
    named = jnp.sum(hit, axis=1)
    before = jnp.cumsum(named, axis=0) - named
    rank = jnp.sum(hit * before[:, None, :], axis=2)
    slot = jnp.sum(hit * placement, axis=2)
    row_index = ((slot ^ me) * capacity + rank).T

    def move(sent, offsets):
        return [
            lax.ppermute(rows, CHIPS, [(i, i ^ offset) for i in range(chips)]) if offset else rows
            for rows, offset in zip(sent, offsets)
        ]

    def work(got_tokens, got_upstream, weights):
        blocks = len(got_tokens)
        return expert(
            jnp.concatenate(got_tokens), jnp.concatenate(got_upstream), *weights, blocks
        )

    def combine(back, offsets):
        rows = jnp.arange(capacity, dtype=jnp.int32)
        hits = jnp.concatenate(
            [(rows + o * capacity)[:, None, None] == row_index[None] for o in offsets]
        )
        weighted = jnp.sum(jnp.where(hits, gates.T[None], 0.0), axis=1).T
        high = weighted.astype(BF16)
        low = (weighted - high.astype(F32)).astype(BF16)
        rows = jnp.concatenate(back)
        part = rows[:, width].astype(F32)
        rows = rows[:, :width]
        return nn(high, rows) + nn(low, rows), jnp.sum(
            jnp.where(hits, part[:, None, None], 0.0), axis=0
        ).T

    half = chips // 2
    near = list(range(half))
    far1, far2 = list(range(half, half + half // 2)), list(range(half + half // 2, chips))
    side = list(range(half // 2))
    cross = list(range(half // 2, half))
    tie = lax.optimization_barrier
    weights = ((w_gate, w_up, w_down), tuple(swap_cores(piece) for piece in (w_gate, w_up, w_down)))

    mirror_tokens = move([tokens], [half])[0]
    sent = dispatch(row_index, [tokens, upstream], near, capacity)
    sent_far = [rows[0] for rows in dispatch(row_index, [upstream], far1 + far2, capacity)]
    sent_side, sent_cross = sent[: len(side)], sent[len(side) :]
    sent_side, index, weights = tie((sent_side, row_index, weights))
    cut = len(cross) // 2
    got_side = move(sent_side, side)
    got_cross = move(sent_cross[:cut], cross[:cut])
    mirror_index = move([index], [half])[0]

    first_up, mirror_tokens = tie((sent_far[:cut], mirror_tokens))
    up_far1 = move(first_up, far1[:cut])
    mirror_tokens, mirror_index, got_cross, got_side, sent_last, rest_up = tie(
        (mirror_tokens, mirror_index, got_cross, got_side, sent_cross[cut:], sent_far[cut:])
    )
    up_far1 += move(rest_up[: len(far1) - cut], far1[cut:])
    sent_far = rest_up[len(far1) - cut :]
    passed = [rows[0] for rows in dispatch(mirror_index, [mirror_tokens], far1 + far2, capacity)]
    pass_far1 = move(passed[: len(far1)], side)
    got_cross += move(sent_last, cross[cut:])
    up_far1, sent_far = tie((up_far1, sent_far))
    up_far2 = move(sent_far, far2)
    pass_far2 = move(passed[len(far1) :], cross)
    up_far1, pass_far1, got_side, got_cross = tie((up_far1, pass_far1, got_side, got_cross))
    got = got_side + got_cross
    first = work(
        pass_far1 + [rows[0] for rows in got], up_far1 + [rows[1] for rows in got], weights
    )
    up_far2, pass_far2, first = tie((up_far2, pass_far2, first))
    back_far1 = move(first[: len(far1)], far1)
    back_near = move(first[len(far1) :], near)
    second = work(pass_far2, up_far2, weights)
    second, back_first = tie((second, back_far1[0]))
    back_far1 = [back_first] + back_far1[1:]
    back_far2 = move(second, far2)
    early, gate_early = combine(back_far1 + back_near, far1 + near)
    late, gate_late = combine(back_far2, far2)
    return (early + late).astype(BF16), gate_early + gate_late


def solution(mesh):
    shape = mesh.devices.shape
    split = Mesh(
        mesh.devices.reshape(shape[0], shape[1], shape[2] // 2, 2), ("rep", "node", "chip", "core")
    )
    return jax.shard_map(
        per_device,
        mesh=split,
        in_specs=(
            P(ROWS, None),
            P(ROWS, None),
            P(ROWS, None),
            P(),
            P(ROWS, None),
            P(PIECES, None, None),
            P(PIECES, None, None),
            P(PIECES, None, None),
        ),
        out_specs=(P(ROWS, None), P(ROWS, None)),
        check_vma=False,
    )
```

```python
import functools

import jax
import jax.numpy as jnp
from jax import lax
from jax.experimental import pallas as pl
from jax.experimental.pallas import tpu as pltpu
from jax.sharding import Mesh
from jax.sharding import PartitionSpec as P

BF16 = jnp.bfloat16
F32 = jnp.float32
CHIPS = ("node", "chip")
ROWS = ("rep", "node", "chip", "core")
PIECES = ("node", "chip", "core")
LANES = 128
VMEM = pl.BlockSpec(memory_space=pltpu.VMEM)
SMALL = pl.CostEstimate(flops=1, bytes_accessed=1, transcendentals=0)


def nt(left, right):
    return lax.dot_general(left, right, (((1,), (1,)), ((), ())), preferred_element_type=F32)


def nn(left, right):
    return jnp.dot(left, right, preferred_element_type=F32)


def swap_cores(values):
    return lax.ppermute(values, "core", [(0, 1), (1, 0)])


def dispatch_kernel(offsets, capacity, index_ref, *refs):
    sources, out_refs = refs[: -len(offsets)], refs[-len(offsets) :]
    count = index_ref.shape[1]
    for offset, out_ref in zip(offsets, out_refs):
        rows = lax.broadcasted_iota(jnp.int32, (capacity, count), 0) + offset * capacity
        hits = jnp.zeros((capacity, count), F32)
        for choice in range(index_ref.shape[0]):
            hits = hits + jnp.where(rows == index_ref[choice : choice + 1, :], 1.0, 0.0)
        hits = hits.astype(BF16)
        for place, source in enumerate(sources):
            out_ref[place] = nn(hits, source[...]).astype(BF16)


def dispatch(row_index, sources, offsets, capacity):
    width = sources[0].shape[1]
    shape = (len(sources), capacity, width)
    return pl.pallas_call(
        functools.partial(dispatch_kernel, offsets, capacity),
        out_shape=[jax.ShapeDtypeStruct(shape, BF16)] * len(offsets),
        in_specs=[VMEM] * (1 + len(sources)),
        out_specs=[VMEM] * len(offsets),
        compiler_params=pltpu.CompilerParams(vmem_limit_bytes=48 << 20),
        cost_estimate=SMALL,
        name="dispatch",
    )(row_index, *sources)


def expert_kernel(tile, tokens_ref, upstream_ref, *refs):
    pieces, out_refs, (total, part) = (refs[:3], refs[3:6]), refs[6:-2], refs[-2:]
    width = tokens_ref.shape[1]
    total[...] = jnp.zeros_like(total)
    part[...] = jnp.zeros_like(part)
    for gate_ref, up_ref, down_ref in pieces:
        for start in range(0, gate_ref.shape[2], tile):
            units = slice(start, start + tile)
            tokens = tokens_ref[...]
            gate_piece, up_piece = gate_ref[0, :, units], up_ref[0, :, units]
            gate_lin = nn(tokens, gate_piece)
            up_lin = nn(tokens, up_piece)
            projected = nt(upstream_ref[...], down_ref[0, units, :])
            sigmoid_g = jax.nn.sigmoid(gate_lin)
            activated = gate_lin * sigmoid_g
            hidden = (activated * up_lin).astype(BF16).astype(F32)
            part[...] += jnp.sum(projected * hidden, axis=1, keepdims=True)
            slope = sigmoid_g * (1.0 + gate_lin * (1.0 - sigmoid_g))
            d_gate = (projected * up_lin * slope).astype(BF16)
            d_up = (projected * activated).astype(BF16)
            total[...] += nt(d_gate, gate_piece) + nt(d_up, up_piece)
    for place, out_ref in enumerate(out_refs):
        count = out_ref.shape[0]
        rows = slice(place * count, (place + 1) * count)
        out_ref[:, :width] = total[rows, :].astype(BF16)
        out_ref[:, width:] = jnp.broadcast_to(part[rows, :], (count, LANES)).astype(BF16)


def expert(tokens, upstream, own, other, blocks):
    rows, width = tokens.shape
    return pl.pallas_call(
        functools.partial(expert_kernel, min(256, own[0].shape[2])),
        out_shape=[jax.ShapeDtypeStruct((rows // blocks, width + LANES), BF16)] * blocks,
        in_specs=[VMEM] * 8,
        out_specs=[VMEM] * blocks,
        scratch_shapes=[pltpu.VMEM((rows, width), F32), pltpu.VMEM((rows, 1), F32)],
        compiler_params=pltpu.CompilerParams(vmem_limit_bytes=38 << 20),
        cost_estimate=SMALL,
        name="expert",
    )(tokens, upstream, *own, *other)


def per_device(tokens, routes, gates, placement, upstream, w_gate, w_up, w_down):
    tok_dev, width = tokens.shape
    top_count = routes.shape[1]
    experts = placement.shape[0]
    nodes, node_chips = lax.axis_size("node"), lax.axis_size("chip")
    chips = nodes * node_chips
    assert chips == experts and chips & (chips - 1) == 0 and nodes % 4 == 0
    capacity = 5 * tok_dev * top_count // (4 * experts)
    me = lax.axis_index("node") * node_chips + lax.axis_index("chip")

    hit = (routes[:, :, None] == jnp.arange(experts, dtype=jnp.int32)).astype(jnp.int32)
    named = jnp.sum(hit, axis=1)
    before = jnp.cumsum(named, axis=0) - named
    rank = jnp.sum(hit * before[:, None, :], axis=2)
    slot = jnp.sum(hit * placement, axis=2)
    row_index = ((slot ^ me) * capacity + rank).T

    def move(sent, offsets):
        return [
            lax.ppermute(rows, CHIPS, [(i, i ^ offset) for i in range(chips)]) if offset else rows
            for rows, offset in zip(sent, offsets)
        ]

    def work(got_tokens, got_upstream, weights):
        blocks = len(got_tokens)
        return expert(
            jnp.concatenate(got_tokens), jnp.concatenate(got_upstream), *weights, blocks
        )

    def combine(back, offsets):
        rows = jnp.arange(capacity, dtype=jnp.int32)
        hits = jnp.concatenate(
            [(rows + o * capacity)[:, None, None] == row_index[None] for o in offsets]
        )
        weighted = jnp.sum(jnp.where(hits, gates.T[None], 0.0), axis=1).T.astype(BF16)
        rows = jnp.concatenate(back)
        part = rows[:, width].astype(F32)
        return nn(weighted, rows[:, :width]), jnp.sum(
            jnp.where(hits, part[:, None, None], 0.0), axis=0
        )

    half = chips // 2
    near = list(range(half))
    far1, far2 = list(range(half, half + half // 2)), list(range(half + half // 2, chips))
    side = list(range(half // 2))
    cross = list(range(half // 2, half))
    tie = lax.optimization_barrier
    weights = ((w_gate, w_up, w_down), tuple(swap_cores(piece) for piece in (w_gate, w_up, w_down)))

    mirror_tokens = move([tokens], [half])[0]
    sent = dispatch(row_index, [tokens, upstream], near, capacity)
    sent_far = [rows[0] for rows in dispatch(row_index, [upstream], far1 + far2, capacity)]
    sent_side, sent_cross = sent[: len(side)], sent[len(side) :]
    sent_side, index, weights = tie((sent_side, row_index, weights))
    cut = len(cross) // 2
    got_side = move(sent_side, side)
    got_cross = move(sent_cross[:cut], cross[:cut])
    mirror_index = move([index], [half])[0]

    first_up, mirror_tokens = tie((sent_far[:cut], mirror_tokens))
    up_far1 = move(first_up, far1[:cut])
    mirror_tokens, mirror_index, got_cross, got_side, sent_last, rest_up = tie(
        (mirror_tokens, mirror_index, got_cross, got_side, sent_cross[cut:], sent_far[cut:])
    )
    up_far1 += move(rest_up[: len(far1) - cut], far1[cut:])
    sent_far = rest_up[len(far1) - cut :]
    passed = [rows[0] for rows in dispatch(mirror_index, [mirror_tokens], far1 + far2, capacity)]
    pass_far1 = move(passed[: len(far1)], side)
    got_last = move(sent_last, cross[cut:])
    got = got_side + got_cross
    zero = work([rows[0] for rows in got], [rows[1] for rows in got], weights)
    passed, zero = tie((passed[len(far1) :], zero))
    pass_far2 = move(passed, cross)

    up_far1, sent_far = tie((up_far1, sent_far))
    up_far2 = move(sent_far, far2)
    up_far1, pass_far1, got_last = tie((up_far1, pass_far1, got_last))
    first = work(
        pass_far1 + [rows[0] for rows in got_last], up_far1 + [rows[1] for rows in got_last], weights
    )
    up_far2, pass_far2, later, zero = tie((up_far2, pass_far2, first, zero))
    first = first[: len(far1)] + later[len(far1) :]

    back_far1 = move(first[: len(far1)], far1)
    back_near = move(zero + first[len(far1) :], near)
    second = work(pass_far2, up_far2, weights)
    second, back_first = tie((second, back_far1[0]))
    back_far1 = [back_first] + back_far1[1:]
    back_far2 = move(second, far2)
    early, gate_early = combine(back_far1 + back_near, far1 + near)
    late, gate_late = combine(back_far2, far2)
    return (early + late).astype(BF16), (gate_early + gate_late).T


def solution(mesh):
    shape = mesh.devices.shape
    split = Mesh(
        mesh.devices.reshape(shape[0], shape[1], shape[2] // 2, 2), ("rep", "node", "chip", "core")
    )
    return jax.shard_map(
        per_device,
        mesh=split,
        in_specs=(
            P(ROWS, None),
            P(ROWS, None),
            P(ROWS, None),
            P(),
            P(ROWS, None),
            P(PIECES, None, None),
            P(PIECES, None, None),
            P(PIECES, None, None),
        ),
        out_specs=(P(ROWS, None), P(ROWS, None)),
        check_vma=False,
    )
```

```python
import functools

import jax
import jax.numpy as jnp
from jax import lax
from jax.experimental import pallas as pl
from jax.experimental.pallas import tpu as pltpu
from jax.sharding import Mesh
from jax.sharding import PartitionSpec as P

BF16 = jnp.bfloat16
F32 = jnp.float32
CHIPS = ("node", "chip")
ROWS = ("rep", "node", "chip", "core")
PIECES = ("node", "chip", "core")
LANES = 128
VMEM = pl.BlockSpec(memory_space=pltpu.VMEM)
SMALL = pl.CostEstimate(flops=1, bytes_accessed=1, transcendentals=0)


def nt(left, right):
    return lax.dot_general(left, right, (((1,), (1,)), ((), ())), preferred_element_type=F32)


def nn(left, right):
    return jnp.dot(left, right, preferred_element_type=F32)


def swap_cores(values):
    return lax.ppermute(values, "core", [(0, 1), (1, 0)])


def dispatch_kernel(offsets, capacity, index_ref, *refs):
    sources, out_refs = refs[: -len(offsets)], refs[-len(offsets) :]
    count = index_ref.shape[1]
    for offset, out_ref in zip(offsets, out_refs):
        rows = lax.broadcasted_iota(jnp.int32, (capacity, count), 0) + offset * capacity
        hits = jnp.zeros((capacity, count), F32)
        for choice in range(index_ref.shape[0]):
            hits = hits + jnp.where(rows == index_ref[choice : choice + 1, :], 1.0, 0.0)
        hits = hits.astype(BF16)
        for place, source in enumerate(sources):
            out_ref[place] = nn(hits, source[...]).astype(BF16)


def dispatch(row_index, sources, offsets, capacity):
    width = sources[0].shape[1]
    shape = (len(sources), capacity, width)
    return pl.pallas_call(
        functools.partial(dispatch_kernel, offsets, capacity),
        out_shape=[jax.ShapeDtypeStruct(shape, BF16)] * len(offsets),
        in_specs=[VMEM] * (1 + len(sources)),
        out_specs=[VMEM] * len(offsets),
        compiler_params=pltpu.CompilerParams(vmem_limit_bytes=48 << 20),
        cost_estimate=SMALL,
        name="dispatch",
    )(row_index, *sources)


def expert_kernel(tile, tokens_ref, upstream_ref, *refs):
    pieces, out_refs, (total, part) = (refs[:3], refs[3:6]), refs[6:-2], refs[-2:]
    width = tokens_ref.shape[1]
    total[...] = jnp.zeros_like(total)
    part[...] = jnp.zeros_like(part)
    for gate_ref, up_ref, down_ref in pieces:
        for start in range(0, gate_ref.shape[2], tile):
            units = slice(start, start + tile)
            tokens = tokens_ref[...]
            gate_piece, up_piece = gate_ref[0, :, units], up_ref[0, :, units]
            gate_lin = nn(tokens, gate_piece)
            up_lin = nn(tokens, up_piece)
            projected = nt(upstream_ref[...], down_ref[0, units, :])
            sigmoid_g = jax.nn.sigmoid(gate_lin)
            activated = gate_lin * sigmoid_g
            hidden = (activated * up_lin).astype(BF16).astype(F32)
            part[...] += jnp.sum(projected * hidden, axis=1, keepdims=True)
            slope = sigmoid_g * (1.0 + gate_lin * (1.0 - sigmoid_g))
            d_gate = (projected * up_lin * slope).astype(BF16)
            d_up = (projected * activated).astype(BF16)
            total[...] += nt(d_gate, gate_piece) + nt(d_up, up_piece)
    for place, out_ref in enumerate(out_refs):
        count = out_ref.shape[0]
        rows = slice(place * count, (place + 1) * count)
        out_ref[:, :width] = total[rows, :].astype(BF16)
        out_ref[:, width:] = jnp.broadcast_to(part[rows, :], (count, LANES)).astype(BF16)


def expert(tokens, upstream, own, other, blocks):
    rows, width = tokens.shape
    return pl.pallas_call(
        functools.partial(expert_kernel, min(256, own[0].shape[2])),
        out_shape=[jax.ShapeDtypeStruct((rows // blocks, width + LANES), BF16)] * blocks,
        in_specs=[VMEM] * 8,
        out_specs=[VMEM] * blocks,
        scratch_shapes=[pltpu.VMEM((rows, width), F32), pltpu.VMEM((rows, 1), F32)],
        compiler_params=pltpu.CompilerParams(vmem_limit_bytes=38 << 20),
        cost_estimate=SMALL,
        name="expert",
    )(tokens, upstream, *own, *other)


def finish_kernel(early_ref, gate_early_ref, weighted_ref, rows_ref, gate_ref, out_ref, sums_ref):
    width = out_ref.shape[1]
    total = early_ref[...] + nn(weighted_ref[...], rows_ref[:, :width])
    out_ref[...] = total.astype(BF16)
    sums_ref[...] = gate_early_ref[...] + gate_ref[...]


def finish(early, gate_early, weighted, rows, gate_late):
    return pl.pallas_call(
        finish_kernel,
        out_shape=[
            jax.ShapeDtypeStruct(early.shape, BF16),
            jax.ShapeDtypeStruct(gate_early.shape, F32),
        ],
        in_specs=[VMEM] * 5,
        out_specs=[VMEM] * 2,
        compiler_params=pltpu.CompilerParams(vmem_limit_bytes=24 << 20),
        cost_estimate=SMALL,
        name="finish",
    )(early, gate_early, weighted, rows, gate_late)


def per_device(tokens, routes, gates, placement, upstream, w_gate, w_up, w_down):
    tok_dev, width = tokens.shape
    top_count = routes.shape[1]
    experts = placement.shape[0]
    nodes, node_chips = lax.axis_size("node"), lax.axis_size("chip")
    chips = nodes * node_chips
    assert chips == experts and chips & (chips - 1) == 0 and nodes % 4 == 0
    capacity = 5 * tok_dev * top_count // (4 * experts)
    me = lax.axis_index("node") * node_chips + lax.axis_index("chip")

    hit = (routes[:, :, None] == jnp.arange(experts, dtype=jnp.int32)).astype(jnp.int32)
    named = jnp.sum(hit, axis=1)
    before = jnp.cumsum(named, axis=0) - named
    rank = jnp.sum(hit * before[:, None, :], axis=2)
    slot = jnp.sum(hit * placement, axis=2)
    row_index = ((slot ^ me) * capacity + rank).T

    def move(sent, offsets):
        return [
            lax.ppermute(rows, CHIPS, [(i, i ^ offset) for i in range(chips)]) if offset else rows
            for rows, offset in zip(sent, offsets)
        ]

    def work(got_tokens, got_upstream, weights):
        blocks = len(got_tokens)
        return expert(
            jnp.concatenate(got_tokens), jnp.concatenate(got_upstream), *weights, blocks
        )

    def combine(back, offsets):
        rows = jnp.arange(capacity, dtype=jnp.int32)
        hits = jnp.concatenate(
            [(rows + o * capacity)[:, None, None] == row_index[None] for o in offsets]
        )
        weighted = jnp.sum(jnp.where(hits, gates.T[None], 0.0), axis=1).T.astype(BF16)
        rows = jnp.concatenate(back)
        part = rows[:, width].astype(F32)
        return weighted, rows, jnp.sum(jnp.where(hits, part[:, None, None], 0.0), axis=0)

    half = chips // 2
    near = list(range(half))
    far1, far2 = list(range(half, half + half // 2)), list(range(half + half // 2, chips))
    side = list(range(half // 2))
    cross = list(range(half // 2, half))
    tie = lax.optimization_barrier
    weights = ((w_gate, w_up, w_down), tuple(swap_cores(piece) for piece in (w_gate, w_up, w_down)))

    mirror_tokens = move([tokens], [half])[0]
    sent = dispatch(row_index, [tokens, upstream], near, capacity)
    sent_far = [rows[0] for rows in dispatch(row_index, [upstream], far1 + far2, capacity)]
    sent_side, sent_cross = sent[: len(side)], sent[len(side) :]
    sent_side, index, weights = tie((sent_side, row_index, weights))
    cut = len(cross) // 2
    got_side = move(sent_side, side)
    got_cross = move(sent_cross[:cut], cross[:cut])
    mirror_index = move([index], [half])[0]

    first_up, mirror_tokens = tie((sent_far[:cut], mirror_tokens))
    up_far1 = move(first_up, far1[:cut])
    mirror_tokens, mirror_index, got_cross, got_side, sent_last, rest_up = tie(
        (mirror_tokens, mirror_index, got_cross, got_side, sent_cross[cut:], sent_far[cut:])
    )
    up_far1 += move(rest_up[: len(far1) - cut], far1[cut:])
    sent_far = rest_up[len(far1) - cut :]
    passed = [rows[0] for rows in dispatch(mirror_index, [mirror_tokens], far1 + far2, capacity)]
    pass_far1 = move(passed[: len(far1)], side)
    got_last = move(sent_last, cross[cut:])
    got = got_side + got_cross
    zero = work([rows[0] for rows in got], [rows[1] for rows in got], weights)
    passed, zero = tie((passed[len(far1) :], zero))
    pass_far2 = move(passed, cross)

    up_far1, sent_far = tie((up_far1, sent_far))
    up_far2 = move(sent_far, far2)
    up_far1, pass_far1, got_last = tie((up_far1, pass_far1, got_last))
    first = work(
        pass_far1 + [rows[0] for rows in got_last], up_far1 + [rows[1] for rows in got_last], weights
    )
    up_far2, pass_far2, later, zero = tie((up_far2, pass_far2, first, zero))
    first = first[: len(far1)] + later[len(far1) :]

    back_far1 = move(first[: len(far1)], far1)
    back_near = move(zero + first[len(far1) :], near)
    second = work(pass_far2, up_far2, weights)
    second, back_first = tie((second, back_far1[0]))
    back_far1 = [back_first] + back_far1[1:]
    back_far2 = move(second, far2)
    back_far1, back_near, ahead = tie((back_far1, back_near, back_far2[:1]))
    back_far2 = ahead + back_far2[1:]
    weighted, rows, gate_early = combine(back_far1 + back_near, far1 + near)
    early = nn(weighted, rows[:, :width])
    weighted, rows, gate_late = combine(back_far2, far2)
    grad_tokens, grad_gates = finish(early, gate_early, weighted, rows, gate_late)
    return grad_tokens, grad_gates.T


def solution(mesh):
    shape = mesh.devices.shape
    split = Mesh(
        mesh.devices.reshape(shape[0], shape[1], shape[2] // 2, 2), ("rep", "node", "chip", "core")
    )
    return jax.shard_map(
        per_device,
        mesh=split,
        in_specs=(
            P(ROWS, None),
            P(ROWS, None),
            P(ROWS, None),
            P(),
            P(ROWS, None),
            P(PIECES, None, None),
            P(PIECES, None, None),
            P(PIECES, None, None),
        ),
        out_specs=(P(ROWS, None), P(ROWS, None)),
        check_vma=False,
    )
```

```python
import functools

import jax
import jax.numpy as jnp
from jax import lax
from jax.experimental import pallas as pl
from jax.experimental.pallas import tpu as pltpu
from jax.sharding import Mesh
from jax.sharding import PartitionSpec as P

BF16 = jnp.bfloat16
F32 = jnp.float32
CHIPS = ("node", "chip")
ROWS = ("rep", "node", "chip", "core")
PIECES = ("node", "chip", "core")
LANES = 128
VMEM = pl.BlockSpec(memory_space=pltpu.VMEM)
SMALL = pl.CostEstimate(flops=1, bytes_accessed=1, transcendentals=0)


def nt(left, right):
    return lax.dot_general(left, right, (((1,), (1,)), ((), ())), preferred_element_type=F32)


def nn(left, right):
    return jnp.dot(left, right, preferred_element_type=F32)


def swap_cores(values):
    return lax.ppermute(values, "core", [(0, 1), (1, 0)])


def dispatch_kernel(offsets, capacity, index_ref, *refs):
    sources, out_refs = refs[: -len(offsets)], refs[-len(offsets) :]
    count = index_ref.shape[1]
    for offset, out_ref in zip(offsets, out_refs):
        rows = lax.broadcasted_iota(jnp.int32, (capacity, count), 0) + offset * capacity
        hits = jnp.zeros((capacity, count), F32)
        for choice in range(index_ref.shape[0]):
            hits = hits + jnp.where(rows == index_ref[choice : choice + 1, :], 1.0, 0.0)
        hits = hits.astype(BF16)
        for place, source in enumerate(sources):
            out_ref[place] = nn(hits, source[...]).astype(BF16)


def dispatch(row_index, sources, offsets, capacity):
    width = sources[0].shape[1]
    shape = (len(sources), capacity, width)
    return pl.pallas_call(
        functools.partial(dispatch_kernel, offsets, capacity),
        out_shape=[jax.ShapeDtypeStruct(shape, BF16)] * len(offsets),
        in_specs=[VMEM] * (1 + len(sources)),
        out_specs=[VMEM] * len(offsets),
        compiler_params=pltpu.CompilerParams(vmem_limit_bytes=48 << 20),
        cost_estimate=SMALL,
        name="dispatch",
    )(row_index, *sources)


def expert_kernel(tile, tokens_ref, upstream_ref, *refs):
    pieces, out_refs, (total, part) = (refs[:3], refs[3:6]), refs[6:-2], refs[-2:]
    width = tokens_ref.shape[1]
    total[...] = jnp.zeros_like(total)
    part[...] = jnp.zeros_like(part)
    for gate_ref, up_ref, down_ref in pieces:
        for start in range(0, gate_ref.shape[2], tile):
            units = slice(start, start + tile)
            tokens = tokens_ref[...]
            gate_piece, up_piece = gate_ref[0, :, units], up_ref[0, :, units]
            gate_lin = nn(tokens, gate_piece)
            up_lin = nn(tokens, up_piece)
            projected = nt(upstream_ref[...], down_ref[0, units, :])
            sigmoid_g = jax.nn.sigmoid(gate_lin)
            activated = gate_lin * sigmoid_g
            hidden = (activated * up_lin).astype(BF16).astype(F32)
            part[...] += jnp.sum(projected * hidden, axis=1, keepdims=True)
            slope = sigmoid_g * (1.0 + gate_lin * (1.0 - sigmoid_g))
            d_gate = (projected * up_lin * slope).astype(BF16)
            d_up = (projected * activated).astype(BF16)
            total[...] += nt(d_gate, gate_piece) + nt(d_up, up_piece)
    for place, out_ref in enumerate(out_refs):
        count = out_ref.shape[0]
        rows = slice(place * count, (place + 1) * count)
        out_ref[:, :width] = total[rows, :].astype(BF16)
        out_ref[:, width:] = jnp.broadcast_to(part[rows, :], (count, LANES)).astype(BF16)


def expert(tokens, upstream, own, other, blocks):
    rows, width = tokens.shape
    return pl.pallas_call(
        functools.partial(expert_kernel, min(512, own[0].shape[2])),
        out_shape=[jax.ShapeDtypeStruct((rows // blocks, width + LANES), BF16)] * blocks,
        in_specs=[VMEM] * 8,
        out_specs=[VMEM] * blocks,
        scratch_shapes=[pltpu.VMEM((rows, width), F32), pltpu.VMEM((rows, 1), F32)],
        compiler_params=pltpu.CompilerParams(vmem_limit_bytes=38 << 20),
        cost_estimate=SMALL,
        name="expert",
    )(tokens, upstream, *own, *other)


def finish_kernel(early_ref, gate_early_ref, weighted_ref, rows_ref, gate_ref, out_ref, sums_ref):
    width = out_ref.shape[1]
    total = early_ref[...] + nn(weighted_ref[...], rows_ref[:, :width])
    out_ref[...] = total.astype(BF16)
    sums_ref[...] = gate_early_ref[...] + gate_ref[...]


def finish(early, gate_early, weighted, rows, gate_late):
    return pl.pallas_call(
        finish_kernel,
        out_shape=[
            jax.ShapeDtypeStruct(early.shape, BF16),
            jax.ShapeDtypeStruct(gate_early.shape, F32),
        ],
        in_specs=[VMEM] * 5,
        out_specs=[VMEM] * 2,
        compiler_params=pltpu.CompilerParams(vmem_limit_bytes=24 << 20),
        cost_estimate=SMALL,
        name="finish",
    )(early, gate_early, weighted, rows, gate_late)


def per_device(tokens, routes, gates, placement, upstream, w_gate, w_up, w_down):
    tok_dev, width = tokens.shape
    top_count = routes.shape[1]
    experts = placement.shape[0]
    nodes, node_chips = lax.axis_size("node"), lax.axis_size("chip")
    chips = nodes * node_chips
    assert chips == experts and chips & (chips - 1) == 0 and nodes % 4 == 0
    capacity = 5 * tok_dev * top_count // (4 * experts)
    me = lax.axis_index("node") * node_chips + lax.axis_index("chip")

    hit = (routes[:, :, None] == jnp.arange(experts, dtype=jnp.int32)).astype(jnp.int32)
    named = jnp.sum(hit, axis=1)
    before = jnp.cumsum(named, axis=0) - named
    rank = jnp.sum(hit * before[:, None, :], axis=2)
    slot = jnp.sum(hit * placement, axis=2)
    row_index = ((slot ^ me) * capacity + rank).T

    def move(sent, offsets):
        return [
            lax.ppermute(rows, CHIPS, [(i, i ^ offset) for i in range(chips)]) if offset else rows
            for rows, offset in zip(sent, offsets)
        ]

    def work(got_tokens, got_upstream, weights):
        blocks = len(got_tokens)
        return expert(
            jnp.concatenate(got_tokens), jnp.concatenate(got_upstream), *weights, blocks
        )

    def combine(back, offsets):
        rows = jnp.arange(capacity, dtype=jnp.int32)
        hits = jnp.concatenate(
            [(rows + o * capacity)[:, None, None] == row_index[None] for o in offsets]
        )
        weighted = jnp.sum(jnp.where(hits, gates.T[None], 0.0), axis=1).T.astype(BF16)
        rows = jnp.concatenate(back)
        part = rows[:, width].astype(F32)
        return weighted, rows, jnp.sum(jnp.where(hits, part[:, None, None], 0.0), axis=0)

    half = chips // 2
    near = list(range(half))
    far1, far2 = list(range(half, half + half // 2)), list(range(half + half // 2, chips))
    side = list(range(half // 2))
    cross = list(range(half // 2, half))
    tie = lax.optimization_barrier
    weights = ((w_gate, w_up, w_down), tuple(swap_cores(piece) for piece in (w_gate, w_up, w_down)))

    mirror_tokens = move([tokens], [half])[0]
    sent = dispatch(row_index, [tokens, upstream], near, capacity)
    sent_far = [rows[0] for rows in dispatch(row_index, [upstream], far1 + far2, capacity)]
    sent_side, sent_cross = sent[: len(side)], sent[len(side) :]
    sent_side, index, weights = tie((sent_side, row_index, weights))
    cut = len(cross) // 2
    got_side = move(sent_side, side)
    got_cross = move(sent_cross[:cut], cross[:cut])
    mirror_index = move([index], [half])[0]

    first_up, mirror_tokens = tie((sent_far[:cut], mirror_tokens))
    up_far1 = move(first_up, far1[:cut])
    mirror_tokens, mirror_index, got_cross, got_side, sent_last, rest_up = tie(
        (mirror_tokens, mirror_index, got_cross, got_side, sent_cross[cut:], sent_far[cut:])
    )
    up_far1 += move(rest_up[: len(far1) - cut], far1[cut:])
    sent_far = rest_up[len(far1) - cut :]
    passed = [rows[0] for rows in dispatch(mirror_index, [mirror_tokens], far1 + far2, capacity)]
    pass_far1 = move(passed[: len(far1)], side)
    got_last = move(sent_last, cross[cut:])
    got = got_side + got_cross
    zero = work([rows[0] for rows in got], [rows[1] for rows in got], weights)
    passed, zero = tie((passed[len(far1) :], zero))
    pass_far2 = move(passed[:cut], cross[:cut])

    up_far1, sent_far, passed = tie((up_far1, sent_far, passed[cut:]))
    pass_far2 = pass_far2 + move(passed, cross[cut:])
    up_far2 = move(sent_far, far2)
    up_far1, pass_far1, got_last = tie((up_far1, pass_far1, got_last))
    first = work(
        pass_far1 + [rows[0] for rows in got_last], up_far1 + [rows[1] for rows in got_last], weights
    )
    up_far2, pass_far2, later, zero = tie((up_far2, pass_far2, first, zero))
    first = first[: len(far1)] + later[len(far1) :]

    back_far1 = move(first[: len(far1)], far1)
    back_near = move(zero + first[len(far1) :], near)
    second = work(pass_far2, up_far2, weights)
    second, back_first = tie((second, back_far1[0]))
    back_far1 = [back_first] + back_far1[1:]
    back_far2 = move(second, far2)
    back_far1, back_near, ahead = tie((back_far1, back_near, back_far2[:1]))
    back_far2 = ahead + back_far2[1:]
    weighted, rows, gate_early = combine(back_far1 + back_near, far1 + near)
    early = nn(weighted, rows[:, :width])
    weighted, rows, gate_late = combine(back_far2, far2)
    grad_tokens, grad_gates = finish(early, gate_early, weighted, rows, gate_late)
    return grad_tokens, grad_gates.T


def solution(mesh):
    shape = mesh.devices.shape
    split = Mesh(
        mesh.devices.reshape(shape[0], shape[1], shape[2] // 2, 2), ("rep", "node", "chip", "core")
    )
    return jax.shard_map(
        per_device,
        mesh=split,
        in_specs=(
            P(ROWS, None),
            P(ROWS, None),
            P(ROWS, None),
            P(),
            P(ROWS, None),
            P(PIECES, None, None),
            P(PIECES, None, None),
            P(PIECES, None, None),
        ),
        out_specs=(P(ROWS, None), P(ROWS, None)),
        check_vma=False,
    )
```

```python
import functools

import jax
import jax.numpy as jnp
from jax import lax
from jax.experimental import pallas as pl
from jax.experimental.pallas import tpu as pltpu
from jax.sharding import Mesh
from jax.sharding import PartitionSpec as P

BF16 = jnp.bfloat16
F32 = jnp.float32
CHIPS = ("node", "chip")
ROWS = ("rep", "node", "chip", "core")
PIECES = ("node", "chip", "core")
LANES = 128
VMEM = pl.BlockSpec(memory_space=pltpu.VMEM)
SMALL = pl.CostEstimate(flops=1, bytes_accessed=1, transcendentals=0)


def nt(left, right):
    return lax.dot_general(left, right, (((1,), (1,)), ((), ())), preferred_element_type=F32)


def nn(left, right):
    return jnp.dot(left, right, preferred_element_type=F32)


def swap_cores(values):
    return lax.ppermute(values, "core", [(0, 1), (1, 0)])


def dispatch_kernel(offsets, capacity, index_ref, *refs):
    sources, out_refs = refs[: -len(offsets)], refs[-len(offsets) :]
    count = index_ref.shape[1]
    for offset, out_ref in zip(offsets, out_refs):
        rows = lax.broadcasted_iota(jnp.int32, (capacity, count), 0) + offset * capacity
        hits = jnp.zeros((capacity, count), F32)
        for choice in range(index_ref.shape[0]):
            hits = hits + jnp.where(rows == index_ref[choice : choice + 1, :], 1.0, 0.0)
        hits = hits.astype(BF16)
        for place, source in enumerate(sources):
            out_ref[place] = nn(hits, source[...]).astype(BF16)


def dispatch(row_index, sources, offsets, capacity):
    width = sources[0].shape[1]
    shape = (len(sources), capacity, width)
    return pl.pallas_call(
        functools.partial(dispatch_kernel, offsets, capacity),
        out_shape=[jax.ShapeDtypeStruct(shape, BF16)] * len(offsets),
        in_specs=[VMEM] * (1 + len(sources)),
        out_specs=[VMEM] * len(offsets),
        compiler_params=pltpu.CompilerParams(vmem_limit_bytes=48 << 20),
        cost_estimate=SMALL,
        name="dispatch",
    )(row_index, *sources)


def expert_kernel(tile, tokens_ref, upstream_ref, *refs):
    pieces, out_refs, (total, part) = (refs[:3], refs[3:6]), refs[6:-2], refs[-2:]
    width = tokens_ref.shape[1]
    total[...] = jnp.zeros_like(total)
    part[...] = jnp.zeros_like(part)
    for gate_ref, up_ref, down_ref in pieces:
        for start in range(0, gate_ref.shape[2], tile):
            units = slice(start, start + tile)
            tokens = tokens_ref[...]
            gate_piece, up_piece = gate_ref[0, :, units], up_ref[0, :, units]
            gate_lin = nn(tokens, gate_piece)
            up_lin = nn(tokens, up_piece)
            projected = nt(upstream_ref[...], down_ref[0, units, :])
            sigmoid_g = jax.nn.sigmoid(gate_lin)
            activated = gate_lin * sigmoid_g
            hidden = (activated * up_lin).astype(BF16).astype(F32)
            part[...] += jnp.sum(projected * hidden, axis=1, keepdims=True)
            slope = sigmoid_g * (1.0 + gate_lin * (1.0 - sigmoid_g))
            d_gate = (projected * up_lin * slope).astype(BF16)
            d_up = (projected * activated).astype(BF16)
            total[...] += nt(d_gate, gate_piece) + nt(d_up, up_piece)
    for place, out_ref in enumerate(out_refs):
        count = out_ref.shape[0]
        rows = slice(place * count, (place + 1) * count)
        out_ref[:, :width] = total[rows, :].astype(BF16)
        out_ref[:, width:] = jnp.broadcast_to(part[rows, :], (count, LANES)).astype(BF16)


def expert(tokens, upstream, own, other, blocks):
    rows, width = tokens.shape
    return pl.pallas_call(
        functools.partial(expert_kernel, min(512, own[0].shape[2])),
        out_shape=[jax.ShapeDtypeStruct((rows // blocks, width + LANES), BF16)] * blocks,
        in_specs=[VMEM] * 8,
        out_specs=[VMEM] * blocks,
        scratch_shapes=[pltpu.VMEM((rows, width), F32), pltpu.VMEM((rows, 1), F32)],
        compiler_params=pltpu.CompilerParams(vmem_limit_bytes=38 << 20),
        cost_estimate=SMALL,
        name="expert",
    )(tokens, upstream, *own, *other)


def finish_kernel(early_ref, gate_early_ref, weighted_ref, rows_ref, gate_ref, out_ref, sums_ref):
    width = out_ref.shape[1]
    total = early_ref[...] + nn(weighted_ref[...], rows_ref[:, :width])
    out_ref[...] = total.astype(BF16)
    sums_ref[...] = gate_early_ref[...] + gate_ref[...]


def finish(early, gate_early, weighted, rows, gate_late):
    return pl.pallas_call(
        finish_kernel,
        out_shape=[
            jax.ShapeDtypeStruct(early.shape, BF16),
            jax.ShapeDtypeStruct(gate_early.shape, F32),
        ],
        in_specs=[VMEM] * 5,
        out_specs=[VMEM] * 2,
        compiler_params=pltpu.CompilerParams(vmem_limit_bytes=24 << 20),
        cost_estimate=SMALL,
        name="finish",
    )(early, gate_early, weighted, rows, gate_late)


def per_device(tokens, routes, gates, placement, upstream, w_gate, w_up, w_down):
    tok_dev, width = tokens.shape
    top_count = routes.shape[1]
    experts = placement.shape[0]
    nodes, node_chips = lax.axis_size("node"), lax.axis_size("chip")
    chips = nodes * node_chips
    assert chips == experts and chips & (chips - 1) == 0 and nodes % 4 == 0
    capacity = 5 * tok_dev * top_count // (4 * experts)
    me = lax.axis_index("node") * node_chips + lax.axis_index("chip")

    hit = (routes[:, :, None] == jnp.arange(experts, dtype=jnp.int32)).astype(jnp.int32)
    named = jnp.sum(hit, axis=1)
    before = jnp.cumsum(named, axis=0) - named
    rank = jnp.sum(hit * before[:, None, :], axis=2)
    slot = jnp.sum(hit * placement, axis=2)
    row_index = ((slot ^ me) * capacity + rank).T

    def move(sent, offsets):
        return [
            lax.ppermute(rows, CHIPS, [(i, i ^ offset) for i in range(chips)]) if offset else rows
            for rows, offset in zip(sent, offsets)
        ]

    def work(got_tokens, got_upstream, weights):
        blocks = len(got_tokens)
        return expert(
            jnp.concatenate(got_tokens), jnp.concatenate(got_upstream), *weights, blocks
        )

    def combine(back, offsets):
        rows = jnp.arange(capacity, dtype=jnp.int32)
        hits = jnp.concatenate(
            [(rows + o * capacity)[:, None, None] == row_index[None] for o in offsets]
        )
        weighted = jnp.sum(jnp.where(hits, gates.T[None], 0.0), axis=1).T.astype(BF16)
        rows = jnp.concatenate(back)
        part = rows[:, width].astype(F32)
        return weighted, rows, jnp.sum(jnp.where(hits, part[:, None, None], 0.0), axis=0)

    half = chips // 2
    near = list(range(half))
    far1, far2 = list(range(half, half + half // 2)), list(range(half + half // 2, chips))
    side = list(range(half // 2))
    cross = list(range(half // 2, half))
    tie = lax.optimization_barrier
    weights = ((w_gate, w_up, w_down), tuple(swap_cores(piece) for piece in (w_gate, w_up, w_down)))

    mirror_tokens = move([tokens], [half])[0]
    sent = dispatch(row_index, [tokens, upstream], near, capacity)
    sent_far = [rows[0] for rows in dispatch(row_index, [upstream], far1 + far2, capacity)]
    sent_side, sent_cross = sent[: len(side)], sent[len(side) :]
    sent_side, index, weights = tie((sent_side, row_index, weights))
    cut = len(cross) // 2
    got_side = move(sent_side, side)
    got_cross = move(sent_cross[:cut], cross[:cut])
    mirror_index = move([index], [half])[0]

    first_up, mirror_tokens = tie((sent_far[:cut], mirror_tokens))
    up_far1 = move(first_up, far1[:cut])
    mirror_tokens, mirror_index, got_cross, got_side, sent_last, rest_up = tie(
        (mirror_tokens, mirror_index, got_cross, got_side, sent_cross[cut:], sent_far[cut:])
    )
    up_far1 += move(rest_up[: len(far1) - cut], far1[cut:])
    sent_far = rest_up[len(far1) - cut :]
    passed = [rows[0] for rows in dispatch(mirror_index, [mirror_tokens], far1 + far2, capacity)]
    pass_far1 = move(passed[: len(far1)], side)
    got_last = move(sent_last, cross[cut:])
    got = got_side + got_cross
    zero = work([rows[0] for rows in got], [rows[1] for rows in got], weights)
    sent_far, zero = tie((sent_far, zero))
    passed = passed[len(far1) :]
    up_far1, sent_far, passed = tie((up_far1, sent_far, passed))
    pass_far2 = move(passed, cross)
    up_far2 = move(sent_far, far2)
    up_far1, pass_far1, got_last = tie((up_far1, pass_far1, got_last))
    first = work(
        pass_far1 + [rows[0] for rows in got_last], up_far1 + [rows[1] for rows in got_last], weights
    )
    up_far2, pass_far2, later, zero = tie((up_far2, pass_far2, first, zero))
    first = first[: len(far1)] + later[len(far1) :]

    back_far1 = move(first[: len(far1)], far1)
    back_near = move(zero + first[len(far1) :], near)
    second = work(pass_far2, up_far2, weights)
    second, back_first = tie((second, back_far1[0]))
    back_far1 = [back_first] + back_far1[1:]
    back_far2 = move(second, far2)
    back_far1, back_near, ahead = tie((back_far1, back_near, back_far2[:1]))
    back_far2 = ahead + back_far2[1:]
    weighted, rows, gate_early = combine(back_far1 + back_near, far1 + near)
    early = nn(weighted, rows[:, :width])
    weighted, rows, gate_late = combine(back_far2, far2)
    grad_tokens, grad_gates = finish(early, gate_early, weighted, rows, gate_late)
    return grad_tokens, grad_gates.T


def solution(mesh):
    shape = mesh.devices.shape
    split = Mesh(
        mesh.devices.reshape(shape[0], shape[1], shape[2] // 2, 2), ("rep", "node", "chip", "core")
    )
    return jax.shard_map(
        per_device,
        mesh=split,
        in_specs=(
            P(ROWS, None),
            P(ROWS, None),
            P(ROWS, None),
            P(),
            P(ROWS, None),
            P(PIECES, None, None),
            P(PIECES, None, None),
            P(PIECES, None, None),
        ),
        out_specs=(P(ROWS, None), P(ROWS, None)),
        check_vma=False,
    )
```

```python
import functools

import jax
import jax.numpy as jnp
from jax import lax
from jax.experimental import pallas as pl
from jax.experimental.pallas import tpu as pltpu
from jax.sharding import Mesh
from jax.sharding import PartitionSpec as P

BF16 = jnp.bfloat16
F32 = jnp.float32
CHIPS = ("node", "chip")
ROWS = ("rep", "node", "chip", "core")
PIECES = ("node", "chip", "core")
LANES = 128
VMEM = pl.BlockSpec(memory_space=pltpu.VMEM)
SMALL = pl.CostEstimate(flops=1, bytes_accessed=1, transcendentals=0)


def nt(left, right):
    return lax.dot_general(left, right, (((1,), (1,)), ((), ())), preferred_element_type=F32)


def nn(left, right):
    return jnp.dot(left, right, preferred_element_type=F32)


def swap_cores(values):
    return lax.ppermute(values, "core", [(0, 1), (1, 0)])


def dispatch_kernel(offsets, capacity, index_ref, *refs):
    sources, out_refs = refs[: -len(offsets)], refs[-len(offsets) :]
    count = index_ref.shape[1]
    for offset, out_ref in zip(offsets, out_refs):
        rows = lax.broadcasted_iota(jnp.int32, (capacity, count), 0) + offset * capacity
        hits = jnp.zeros((capacity, count), F32)
        for choice in range(index_ref.shape[0]):
            hits = hits + jnp.where(rows == index_ref[choice : choice + 1, :], 1.0, 0.0)
        hits = hits.astype(BF16)
        for place, source in enumerate(sources):
            out_ref[place] = nn(hits, source[...]).astype(BF16)


def dispatch(row_index, sources, offsets, capacity):
    width = sources[0].shape[1]
    shape = (len(sources), capacity, width)
    return pl.pallas_call(
        functools.partial(dispatch_kernel, offsets, capacity),
        out_shape=[jax.ShapeDtypeStruct(shape, BF16)] * len(offsets),
        in_specs=[VMEM] * (1 + len(sources)),
        out_specs=[VMEM] * len(offsets),
        compiler_params=pltpu.CompilerParams(vmem_limit_bytes=48 << 20),
        cost_estimate=SMALL,
        name="dispatch",
    )(row_index, *sources)


def expert_kernel(tile, tokens_ref, upstream_ref, *refs):
    pieces, out_refs, (total, part) = (refs[:3], refs[3:6]), refs[6:-2], refs[-2:]
    width = tokens_ref.shape[1]
    for gate_ref, up_ref, down_ref in pieces:
        for start in range(0, gate_ref.shape[2], tile):
            units = slice(start, start + tile)
            tokens = tokens_ref[...]
            gate_piece, up_piece = gate_ref[0, :, units], up_ref[0, :, units]
            gate_lin = nn(tokens, gate_piece)
            up_lin = nn(tokens, up_piece)
            projected = nt(upstream_ref[...], down_ref[0, units, :])
            sigmoid_g = jax.nn.sigmoid(gate_lin)
            activated = gate_lin * sigmoid_g
            hidden = (activated * up_lin).astype(BF16).astype(F32)
            parts = jnp.sum(projected * hidden, axis=1, keepdims=True)
            slope = sigmoid_g * (1.0 + gate_lin * (1.0 - sigmoid_g))
            d_gate = (projected * up_lin * slope).astype(BF16)
            d_up = (projected * activated).astype(BF16)
            sums = nt(d_gate, gate_piece) + nt(d_up, up_piece)
            if start == 0 and gate_ref is pieces[0][0]:
                part[...], total[...] = parts, sums
            else:
                part[...] += parts
                total[...] += sums
    for place, out_ref in enumerate(out_refs):
        count = out_ref.shape[0]
        rows = slice(place * count, (place + 1) * count)
        out_ref[:, :width] = total[rows, :].astype(BF16)
        out_ref[:, width:] = jnp.broadcast_to(part[rows, :], (count, LANES)).astype(BF16)


def expert(tokens, upstream, own, other, blocks):
    rows, width = tokens.shape
    return pl.pallas_call(
        functools.partial(expert_kernel, min(512, own[0].shape[2])),
        out_shape=[jax.ShapeDtypeStruct((rows // blocks, width + LANES), BF16)] * blocks,
        in_specs=[VMEM] * 8,
        out_specs=[VMEM] * blocks,
        scratch_shapes=[pltpu.VMEM((rows, width), F32), pltpu.VMEM((rows, 1), F32)],
        compiler_params=pltpu.CompilerParams(vmem_limit_bytes=38 << 20),
        cost_estimate=SMALL,
        name="expert",
    )(tokens, upstream, *own, *other)


def finish_kernel(early_ref, gate_early_ref, weighted_ref, rows_ref, gate_ref, out_ref, sums_ref):
    width = out_ref.shape[1]
    total = early_ref[...] + nn(weighted_ref[...], rows_ref[:, :width])
    out_ref[...] = total.astype(BF16)
    sums_ref[...] = gate_early_ref[...] + gate_ref[...]


def finish(early, gate_early, weighted, rows, gate_late):
    return pl.pallas_call(
        finish_kernel,
        out_shape=[
            jax.ShapeDtypeStruct(early.shape, BF16),
            jax.ShapeDtypeStruct(gate_early.shape, F32),
        ],
        in_specs=[VMEM] * 5,
        out_specs=[VMEM] * 2,
        compiler_params=pltpu.CompilerParams(vmem_limit_bytes=24 << 20),
        cost_estimate=SMALL,
        name="finish",
    )(early, gate_early, weighted, rows, gate_late)


def per_device(tokens, routes, gates, placement, upstream, w_gate, w_up, w_down):
    tok_dev, width = tokens.shape
    top_count = routes.shape[1]
    experts = placement.shape[0]
    nodes, node_chips = lax.axis_size("node"), lax.axis_size("chip")
    chips = nodes * node_chips
    assert chips == experts and chips & (chips - 1) == 0 and nodes % 4 == 0
    capacity = 5 * tok_dev * top_count // (4 * experts)
    me = lax.axis_index("node") * node_chips + lax.axis_index("chip")

    hit = (routes[:, :, None] == jnp.arange(experts, dtype=jnp.int32)).astype(jnp.int32)
    named = jnp.sum(hit, axis=1)
    before = jnp.cumsum(named, axis=0) - named
    rank = jnp.sum(hit * before[:, None, :], axis=2)
    slot = jnp.sum(hit * placement, axis=2)
    row_index = ((slot ^ me) * capacity + rank).T

    def move(sent, offsets):
        return [
            lax.ppermute(rows, CHIPS, [(i, i ^ offset) for i in range(chips)]) if offset else rows
            for rows, offset in zip(sent, offsets)
        ]

    def work(got_tokens, got_upstream, weights):
        blocks = len(got_tokens)
        return expert(
            jnp.concatenate(got_tokens), jnp.concatenate(got_upstream), *weights, blocks
        )

    def combine(back, offsets):
        rows = jnp.arange(capacity, dtype=jnp.int32)
        hits = jnp.concatenate(
            [(rows + o * capacity)[:, None, None] == row_index[None] for o in offsets]
        )
        weighted = jnp.sum(jnp.where(hits, gates.T[None], 0.0), axis=1).T.astype(BF16)
        rows = jnp.concatenate(back)
        part = rows[:, width].astype(F32)
        return weighted, rows, jnp.sum(jnp.where(hits, part[:, None, None], 0.0), axis=0)

    half = chips // 2
    near = list(range(half))
    far1, far2 = list(range(half, half + half // 2)), list(range(half + half // 2, chips))
    side = list(range(half // 2))
    cross = list(range(half // 2, half))
    tie = lax.optimization_barrier
    weights = ((w_gate, w_up, w_down), tuple(swap_cores(piece) for piece in (w_gate, w_up, w_down)))

    mirror_tokens = move([tokens], [half])[0]
    sent = dispatch(row_index, [tokens, upstream], near, capacity)
    sent_far = [rows[0] for rows in dispatch(row_index, [upstream], far1 + far2, capacity)]
    sent_side, sent_cross = sent[: len(side)], sent[len(side) :]
    sent_side, index, weights = tie((sent_side, row_index, weights))
    cut = len(cross) // 2
    got_side = move(sent_side, side)
    got_cross = move(sent_cross[:cut], cross[:cut])
    mirror_index = move([index], [half])[0]

    first_up, mirror_tokens = tie((sent_far[:cut], mirror_tokens))
    up_far1 = move(first_up, far1[:cut])
    mirror_tokens, mirror_index, got_cross, got_side, sent_last, rest_up = tie(
        (mirror_tokens, mirror_index, got_cross, got_side, sent_cross[cut:], sent_far[cut:])
    )
    up_far1 += move(rest_up[: len(far1) - cut], far1[cut:])
    sent_far = rest_up[len(far1) - cut :]
    passed = [rows[0] for rows in dispatch(mirror_index, [mirror_tokens], far1 + far2, capacity)]
    pass_far1 = move(passed[: len(far1)], side)
    got_last = move(sent_last, cross[cut:])
    got = got_side + got_cross
    zero = work([rows[0] for rows in got], [rows[1] for rows in got], weights)
    sent_far, zero = tie((sent_far, zero))
    passed = passed[len(far1) :]
    up_far1, sent_far, passed = tie((up_far1, sent_far, passed))
    pass_far2 = move(passed, cross)
    up_far2 = move(sent_far, far2)
    up_far1, pass_far1, got_last = tie((up_far1, pass_far1, got_last))
    first = work(
        pass_far1 + [rows[0] for rows in got_last], up_far1 + [rows[1] for rows in got_last], weights
    )
    up_far2, pass_far2, later, zero = tie((up_far2, pass_far2, first, zero))
    first = first[: len(far1)] + later[len(far1) :]

    back_far1 = move(first[: len(far1)], far1)
    back_near = move(zero + first[len(far1) :], near)
    second = work(pass_far2, up_far2, weights)
    second, back_first = tie((second, back_far1[0]))
    back_far1 = [back_first] + back_far1[1:]
    back_far2 = move(second, far2)
    back_far1, back_near, ahead = tie((back_far1, back_near, back_far2[:1]))
    back_far2 = ahead + back_far2[1:]
    weighted, rows, gate_early = combine(back_far1 + back_near, far1 + near)
    early = nn(weighted, rows[:, :width])
    weighted, rows, gate_late = combine(back_far2, far2)
    grad_tokens, grad_gates = finish(early, gate_early, weighted, rows, gate_late)
    return grad_tokens, grad_gates.T


def solution(mesh):
    shape = mesh.devices.shape
    split = Mesh(
        mesh.devices.reshape(shape[0], shape[1], shape[2] // 2, 2), ("rep", "node", "chip", "core")
    )
    return jax.shard_map(
        per_device,
        mesh=split,
        in_specs=(
            P(ROWS, None),
            P(ROWS, None),
            P(ROWS, None),
            P(),
            P(ROWS, None),
            P(PIECES, None, None),
            P(PIECES, None, None),
            P(PIECES, None, None),
        ),
        out_specs=(P(ROWS, None), P(ROWS, None)),
        check_vma=False,
    )
```
